32 devices in a mesh: groups: 2 (over y), seq: 8 (over z, x), tp: 2 (over core).
Axes of the slice: x: 2, y: 2, z: 4, core: 2. Of those that a mesh axis runs over, the one named last changes fastest.
Arguments:
- features: bfloat16 [3, 4096, 4096], P(None, 'tp', ('groups', 'seq')), parts along dimension 2, may hold values from -6 to 6
- short_filter: float32 [3, 3, 4096], P(None, None, 'tp'), may hold values from -3.5 to 3.5
- mr_filter: bfloat16 [256, 128], P('tp'), may hold values from -0.5 to 0.5
- mr_bias: float32 [4096], P('tp'), may hold values from -4 to 4
- candidate: int32 [4096], P(('groups', 'seq')), parts along dimension 0, may hold values from 0 to 3, never falling along the last dimension, each value on 1 to 1024 neighbouring positions
Outputs:
- running: bfloat16 [4096, 4096], P('tp', ('groups', 'seq')), parts along dimension 1
The draws below stay inside these ranges and needn't reach their ends.
There are 2 independent parts, one for each index of `groups`. The reference program is written for one: setup_inputs(seed, part) draws one part's arguments, and reference() takes and returns one part's arrays. A program takes and returns all parts, laid end to end along the dimension named above; an argument that names none is the same for every part. Nothing has to cross between parts.
Inputs may be any that keep to these rules, and one draw needn't show every extreme that they name: `candidate`: ids never fall along the stretch; every one of the 4 candidates has 1 to 1024 tokens, and one has exactly 1024.
All inputs are finite; a program needn't handle non-finite values.
Results may differ from the reference program's by a relative error of at most 0.009.
Values may be sent and summed in bfloat16 or wider, within the bound.
A program may use at most 128 MiB of HBM per device.

```python
import math
import jax
import jax.numpy as jnp
import numpy as np
from jax import lax

D = 4096
MR_GROUPS = 256
FLEN = 128
SHORT = 3
NCAND = 4
SEQ_LEN = 2048


def block_scale(rng, dims, pieces, low, high):
    def one(axis_at, shards_of):
        heights = jax.random.uniform(jax.random.fold_in(jax.random.fold_in(rng, 6), axis_at), (shards_of,), jnp.float32, low / len(pieces), high / len(pieces))
        return jnp.repeat(jnp.exp(heights), dims[axis_at] // shards_of).reshape((-1,) + (1,) * (len(dims) - axis_at - 1))

    loudness = one(*pieces[0])
    for cut in pieces[1:]:
        loudness = loudness * one(*cut)
    return loudness


def length_profile(count, total, most, lean):
    portions = [(1 << 20) // math.isqrt(standing ** lean) + 1 for standing in range(2, count + 1)]
    spare, holding = total - most - (count - 1), [1] * (count - 1)
    while spare > 0:
        movable = [i for i in range(count - 1) if holding[i] < most]
        mass, remaining = sum([portions[i] for i in movable]), spare
        for i in movable:
            more = min(most - holding[i], max(1, remaining * portions[i] // mass), spare)
            holding[i] = holding[i] + more
            spare = spare - more
    return np.array([most] + holding)


def uneven_parts(key, count, total, bound, lean):
    if count == 2:
        one = jax.random.randint(key, (), max(1, total - bound), min(bound, total - 1) + 1)
        return jnp.stack([one, total - one])
    lengths = jnp.asarray(length_profile(count, total, bound, lean), jnp.int32)
    pairs = (count - 1) // 2
    source_of, taker = lengths[1:1 + 2 * pairs:2], lengths[2:2 + 2 * pairs:2]
    room = jnp.minimum(source_of - 1, bound - taker)
    moved = jax.random.randint(jax.random.fold_in(key, 1), (pairs,), 0, 1 << 20) % (room + 1)
    lengths = lengths.at[1:1 + 2 * pairs:2].set(source_of - moved).at[2:2 + 2 * pairs:2].set(taker + moved)
    return lengths[jax.random.permutation(jax.random.fold_in(key, 2), count)]


def centred(key, extent, width, limit, shards=(), held_as=jnp.bfloat16):
    loudness = block_scale(key, extent, shards, -0.22, 0.18) if shards else 1.0
    values = jax.random.normal(key, extent, jnp.float32) * width * loudness
    return jnp.minimum(jnp.maximum(values, -limit), limit).astype(held_as)


def setup_inputs(seed: int = 0, part: int = 0) -> dict:
    streams_of = jax.random.split(jax.random.key(seed), 6)
    part_keys = jax.random.split(jax.random.fold_in(streams_of[5], part), 6)
    features = centred(part_keys[0], (3, D, SEQ_LEN), 1.0, 6.0, ((1, 2), (2, 8)))
    short_filter = centred(streams_of[1], (SHORT, 3, D), SHORT ** -0.5, 3.5, ((2, 2),), jnp.float32)
    mr_filter = centred(streams_of[2], (MR_GROUPS, FLEN), FLEN ** -0.5, 0.5, ((0, 2),))
    mr_bias = centred(streams_of[3], (D,), 1.0, 4.0, ((0, 2),), jnp.float32)
    candidate = jnp.searchsorted(jnp.cumsum(uneven_parts(part_keys[4], NCAND, SEQ_LEN, SEQ_LEN // 2, 2)), jnp.arange(SEQ_LEN), side="right").astype(jnp.int32)
    return {"features": features, "short_filter": short_filter, "mr_filter": mr_filter, "mr_bias": mr_bias, "candidate": candidate}


def lagged(values, shift_by, fill):
    padding = jnp.full(values.shape[:-1] + (shift_by,), fill, values.dtype)
    return jnp.concatenate([padding, values[..., :values.shape[-1] - shift_by]], axis=-1)

def reference(features, short_filter, mr_filter, mr_bias, candidate):
    seq_len = features.shape[2]
    inputs = features.astype(jnp.float32)
    owner = candidate.astype(jnp.int32)
    same_one = (lagged(owner, 1, -1) == owner).astype(jnp.float32)
    same_two = (lagged(owner, 2, -1) == owner).astype(jnp.float32)
    short_out = short_filter[0][:, :, None] * inputs + short_filter[1][:, :, None] * (lagged(inputs, 1, 0.0) * same_one) + short_filter[2][:, :, None] * (lagged(inputs, 2, 0.0) * same_two)
    gated = (short_out[1] * short_out[2]).astype(jnp.bfloat16)
    gated_f = gated.astype(jnp.float32)
    filter_taps = jnp.repeat(mr_filter.astype(jnp.float32), D // MR_GROUPS, axis=0)
    padded = jnp.concatenate([jnp.zeros((D, FLEN - 1), jnp.float32), gated_f], axis=1)
    padded_ids = jnp.concatenate([jnp.full((FLEN - 1,), -1, jnp.int32), owner])

    def add_tap(tap_index, accum):
        tap_index = jnp.asarray(tap_index).astype(jnp.int32)
        start = (FLEN - 1 - tap_index).astype(jnp.int32)
        shifted = lax.dynamic_slice_in_dim(padded, start, seq_len, 1)
        shifted_ids = lax.dynamic_slice_in_dim(padded_ids, start, seq_len, 0)
        weight_col = lax.dynamic_slice_in_dim(filter_taps, tap_index, 1, 1)
        return accum + weight_col * (shifted * (shifted_ids == owner).astype(jnp.float32))
    conv = lax.fori_loop(0, FLEN, add_tap, jnp.zeros((D, seq_len), jnp.float32))
    mixed = (short_out[0] * (conv + mr_bias[:, None] * gated_f)).astype(jnp.bfloat16)
    running_sum = jnp.cumsum(mixed.astype(jnp.float32), axis=1)
    member = (owner[:, None] == jnp.arange(NCAND, dtype=jnp.int32)[None, :]).astype(jnp.int32)
    seg_sizes = lax.optimization_barrier(jnp.sum(member, axis=0))
    starts = (jnp.cumsum(seg_sizes) - seg_sizes).astype(jnp.int32)
    before_index = jnp.maximum(starts - 1, 0).astype(jnp.int32)
    before = jnp.where(starts[None, :] > 0, running_sum[:, before_index], 0.0)
    start_tok = starts[owner]
    before_tok = before[:, owner]
    count = (jnp.arange(seq_len, dtype=jnp.int32) - start_tok + 1).astype(jnp.float32)
    return ((running_sum - before_tok) / jnp.sqrt(count)[None, :]).astype(jnp.bfloat16)
```

```python
import functools

import jax
import jax.numpy as jnp
from jax import lax
from jax.experimental import pallas as pl
from jax.experimental.pallas import tpu as pltpu
from jax.sharding import PartitionSpec as P

NCAND = 4
ROWS = 128
LANES = 128
F32 = jnp.float32
BF16 = jnp.bfloat16


def iota(shape, dim):
    return lax.broadcasted_iota(jnp.int32, shape, dim)


def dot(a, b):
    return jnp.dot(a, b, preferred_element_type=F32)


def earlier_ids(ids, own):
    total = jnp.zeros(own.shape, jnp.int32)
    for cand in range(NCAND):
        fewer = jnp.sum((ids < cand).astype(F32), axis=1, keepdims=True).astype(jnp.int32)
        total = jnp.where(own == cand, fewer, total)
    return total


def kernel(
    count, reach,
    x_ref, filt_ref, mr_ref, bias_ref, cand_ref, out_ref,
    rows_ref, prm_ref, mrf_ref, shift_ref, band_ref, pool_ref, table_ref,
    g0_ref, g1_ref, gh_ref, gate_ref, conv_ref, mixsum_ref,
    rim_out, rim_in, ids_in, sums_out, sums_in,
    halo_send, halo_recv, rim_send, rim_recv, ids_send, ids_recv, sums_send, sums_recv,
):
    me = lax.axis_index("seq")
    channels, tokens = out_ref.shape
    chunks = channels // ROWS
    groups = mr_ref.shape[0]
    size = channels // groups
    per_chunk = ROWS // size
    n_to = jnp.minimum(reach, count - 1 - me)
    n_from = jnp.minimum(reach, me)

    def halo_copy(i):
        rows = pl.ds(pl.multiple_of(i * ROWS, ROWS), ROWS)
        return pltpu.make_async_remote_copy(
            src_ref=g1_ref.at[rows], dst_ref=gh_ref.at[rows],
            send_sem=halo_send.at[i], recv_sem=halo_recv.at[i],
            device_id={"seq": me + 1}, device_id_type=pl.DeviceIdType.MESH)

    def rim_copy():
        return pltpu.make_async_remote_copy(
            src_ref=rim_out, dst_ref=rim_in, send_sem=rim_send, recv_sem=rim_recv,
            device_id={"seq": me + 1}, device_id_type=pl.DeviceIdType.MESH)

    def ids_copy(d):
        return pltpu.make_async_remote_copy(
            src_ref=cand_ref, dst_ref=ids_in.at[d - 1],
            send_sem=ids_send.at[d - 1], recv_sem=ids_recv.at[d - 1],
            device_id={"seq": me + d}, device_id_type=pl.DeviceIdType.MESH)

    def sums_copy(d):
        return pltpu.make_async_remote_copy(
            src_ref=sums_out, dst_ref=sums_in.at[d - 1],
            send_sem=sums_send.at[d - 1], recv_sem=sums_recv.at[d - 1],
            device_id={"seq": me + d}, device_id_type=pl.DeviceIdType.MESH)

    def loop(low, high, body):
        def step(i, carry):
            body(i)
            return carry
        lax.fori_loop(low, high, step, 0)

    barrier = pltpu.get_barrier_semaphore()
    loop(1, n_from + 1, lambda d: pl.semaphore_signal(
        barrier, inc=1, device_id={"seq": me - d}, device_id_type=pl.DeviceIdType.MESH))

    own = cand_ref[...]
    start = earlier_ids(own, own)
    k2, t2 = iota((tokens, tokens), 0), iota((tokens, tokens), 1)
    inside = k2 >= start
    band_ref[...] = (inside & (k2 <= t2) & (t2 - k2 < LANES)).astype(F32).astype(BF16)
    pool_ref[...] = (inside & (k2 <= t2)).astype(F32).astype(BF16)
    shift_ref[0] = (inside & (k2 == t2 - 1)).astype(F32).astype(BF16)
    shift_ref[1] = (inside & (k2 == t2 - 2)).astype(F32).astype(BF16)

    row_k, lane_k = iota((16, LANES), 0), iota((16, LANES), 1)
    rim = jnp.zeros((16, channels), F32)
    for b in range(3):
        pick = (lane_k - (LANES - 2) == row_k - 2 * b) & (lane_k >= LANES - 2)
        rim = rim + lax.dot_general(
            pick.astype(F32).astype(BF16), x_ref[b, :, tokens - LANES:],
            (((1,), (1,)), ((), ())), preferred_element_type=F32)
    rim_out[...] = rim.astype(BF16)

    @pl.when(me + 1 < count)
    def _():
        pl.semaphore_wait(barrier, n_to)

    loop(1, n_to + 1, lambda d: ids_copy(d).start())

    @pl.when(me + 1 < count)
    def _():
        rim_copy().start()

    rows_ref[...] = jnp.zeros_like(rows_ref)

    def tail(i):
        rows = pl.ds(pl.multiple_of(i * ROWS, ROWS), ROWS)
        for j in range(3):
            rows_ref[3 * j:3 * j + 3, :] = filt_ref[j, :, rows]
        rows_ref[9:10, :] = bias_ref[:, rows]
        prm = rows_ref[...].T
        prm_ref[rows, :] = prm
        outs = []
        for b in (1, 2):
            x = x_ref[b, rows, :]
            one = dot(x, shift_ref[0, :, LANES:])
            two = dot(x, shift_ref[1, :, LANES:])
            outs.append(prm[:, b:b + 1] * x[:, LANES:].astype(F32)
                        + prm[:, 3 + b:4 + b] * one + prm[:, 6 + b:7 + b] * two)
        g1_ref[rows, :] = (outs[0] * outs[1]).astype(BF16)

        @pl.when(me + 1 < count)
        def _():
            halo_copy(i).start()

    loop(0, chunks, tail)
    mrf_ref[...] = mr_ref[...].astype(F32)

    @pl.when(me == 0)
    def _():
        gh_ref[...] = jnp.zeros_like(gh_ref)
        rim_in[...] = jnp.zeros_like(rim_in)
        ids_in[0] = jnp.full(ids_in.shape[1:], -1, jnp.int32)

    @pl.when(me > 0)
    def _():
        rim_copy().wait_recv()
    loop(1, n_from + 1, lambda d: ids_copy(d).wait_recv())

    start_all = start + earlier_ids(ids_in[0][:, tokens - LANES:], own) - LANES
    kh, th = iota((LANES, LANES), 0), iota((LANES, LANES), 1)
    halo_mask = ((kh > th) & (kh - LANES >= start_all[:, :LANES])).astype(F32).astype(BF16)
    row_q, lane_q = iota((16, LANES), 0), iota((16, LANES), 1)

    def rim_pick(b, lag):
        token = row_q - 2 * b - 2
        hit = (token == lane_q - lag) & (token >= start_all[:, :LANES]) & (token < 0) & (token >= -2)
        return hit.astype(F32).astype(BF16)

    picks = [[rim_pick(b, lag) for lag in (1, 2)] for b in range(3)]

    def head(i):
        rows = pl.ds(pl.multiple_of(i * ROWS, ROWS), ROWS)
        prm = prm_ref[rows, :]
        edge = rim_in[:, rows]
        outs = []
        for b in range(3):
            x = x_ref[b, rows, :]
            lags = [dot(x, shift_ref[j, :, :LANES]) + lax.dot_general(
                edge, picks[b][j], (((0,), (0,)), ((), ())), preferred_element_type=F32)
                for j in range(2)]
            outs.append(prm[:, b:b + 1] * x[:, :LANES].astype(F32)
                        + prm[:, 3 + b:4 + b] * lags[0] + prm[:, 6 + b:7 + b] * lags[1])
        g0_ref[rows, :] = (outs[1] * outs[2]).astype(BF16)
        gate_ref[rows, :LANES] = outs[0]
        x = x_ref[0, rows, :]
        one = dot(x, shift_ref[0, :, LANES:])
        two = dot(x, shift_ref[1, :, LANES:])
        gate_ref[rows, LANES:] = (prm[:, 0:1] * x[:, LANES:].astype(F32)
                                  + prm[:, 3:4] * one + prm[:, 6:7] * two)

    loop(0, chunks, head)

    def conv(i):
        for u in range(4):
            group = i * 4 + u
            rows = pl.ds(pl.multiple_of(group * size, size), size)
            taps = jnp.broadcast_to(mrf_ref[pl.ds(group, 1), :], (LANES, LANES))
            wheel = pltpu.roll(taps, 0, 1, stride=1, stride_axis=0).astype(BF16)
            table_ref[group] = wheel * halo_mask
            upper = jnp.concatenate([wheel, wheel], axis=1) * band_ref[:LANES, :]
            right = wheel * band_ref[LANES:, LANES:]
            near = dot(g0_ref[rows, :], upper)
            conv_ref[rows, :LANES] = near[:, :LANES]
            conv_ref[rows, LANES:] = near[:, LANES:] + dot(g1_ref[rows, :], right)

    loop(0, groups // 4, conv)

    last = jnp.max(own.astype(F32), axis=1, keepdims=True)
    last_of = (iota((tokens, tokens), 0) >= earlier_ids(own, last.astype(jnp.int32)))
    last_col = last_of[:, :LANES].astype(F32)
    lane_p = iota((tokens, LANES), 1)
    mixsum_ref[...] = jnp.zeros_like(mixsum_ref)

    def mix(i):
        rows = pl.ds(pl.multiple_of(i * ROWS, ROWS), ROWS)

        @pl.when(me > 0)
        def _():
            halo_copy(i).wait_recv()

        for u in range(per_chunk):
            group = i * per_chunk + u
            some = pl.ds(pl.multiple_of(group * size, size), size)
            conv_ref[some, :LANES] += dot(gh_ref[some, :], table_ref[group])
        bias = prm_ref[rows, 9:10]
        gated = jnp.concatenate([g0_ref[rows, :], g1_ref[rows, :]], axis=1).astype(F32)
        mixed = (gate_ref[rows, :] * (conv_ref[rows, :] + bias * gated)).astype(BF16)
        conv_ref[rows, :] = dot(mixed, pool_ref[...])
        mixsum_ref[...] += dot(mixed, jnp.where(lane_p == i, last_col, 0.0).astype(BF16))

    loop(0, chunks, mix)

    sums_out[...] = mixsum_ref[...].T[:sums_out.shape[0], :]
    loop(1, n_to + 1, lambda d: sums_copy(d).start())

    first = jnp.min(own.astype(F32), axis=1, keepdims=True).astype(jnp.int32)
    mixsum_ref[...] = jnp.zeros_like(mixsum_ref)

    def gather(d, before):
        sums_copy(d).wait_recv()
        ids = ids_in[d - 1]
        same = jnp.max(ids.astype(F32), axis=1, keepdims=True).astype(jnp.int32) == first
        mixsum_ref[:sums_out.shape[0], :] += jnp.where(same, sums_in[d - 1], 0.0)
        return before + jnp.sum((ids == first).astype(F32), axis=1, keepdims=True)

    before = lax.fori_loop(1, n_from + 1, gather, jnp.zeros((1, 1), F32))
    carried = (start == 0).astype(F32)
    seen = (iota(start.shape, 1) + 1 - start).astype(F32) + carried * before
    scale = 1.0 / jnp.sqrt(seen)
    mixsum_ref[...] = mixsum_ref[...].T

    def finish(i):
        rows = pl.ds(pl.multiple_of(i * ROWS, ROWS), ROWS)
        column = jnp.sum(jnp.where(iota((ROWS, LANES), 1) == i, mixsum_ref[...], 0.0), axis=1, keepdims=True)
        out_ref[rows, :] = ((conv_ref[rows, :] + column * carried) * scale).astype(BF16)

    loop(0, chunks, finish)

    loop(1, n_to + 1, lambda d: sums_copy(d).wait_send())
    loop(1, n_to + 1, lambda d: ids_copy(d).wait_send())

    @pl.when(me + 1 < count)
    def _():
        rim_copy().wait_send()
        loop(0, chunks, lambda i: halo_copy(i).wait_send())


def on_device(features, short_filter, mr_filter, mr_bias, candidate):
    count = lax.axis_size("seq")
    reach = max(1, count // 2)
    _, channels, tokens = features.shape
    groups = mr_filter.shape[0]
    chunks = channels // ROWS
    sum_rows = -(-chunks // 8) * 8
    dma = pltpu.SemaphoreType.DMA
    vmem = pl.BlockSpec(memory_space=pltpu.VMEM)
    return pl.pallas_call(
        functools.partial(kernel, count, reach),
        out_shape=jax.ShapeDtypeStruct((channels, tokens), BF16),
        in_specs=[vmem] * 5,
        out_specs=vmem,
        scratch_shapes=[
            pltpu.VMEM((ROWS, LANES), F32),
            pltpu.VMEM((channels, LANES), F32),
            pltpu.VMEM((groups, LANES), F32),
            pltpu.VMEM((2, tokens, tokens), BF16),
            pltpu.VMEM((tokens, tokens), BF16),
            pltpu.VMEM((tokens, tokens), BF16),
            pltpu.VMEM((groups, LANES, LANES), BF16),
            pltpu.VMEM((channels, LANES), BF16),
            pltpu.VMEM((channels, LANES), BF16),
            pltpu.VMEM((channels, LANES), BF16),
            pltpu.VMEM((channels, tokens), F32),
            pltpu.VMEM((channels, tokens), F32),
            pltpu.VMEM((LANES, LANES), F32),
            pltpu.VMEM((16, channels), BF16),
            pltpu.VMEM((16, channels), BF16),
            pltpu.VMEM((reach, 1, tokens), jnp.int32),
            pltpu.VMEM((sum_rows, LANES), F32),
            pltpu.VMEM((reach, sum_rows, LANES), F32),
            dma((chunks,)), dma((chunks,)), dma, dma,
            dma((reach,)), dma((reach,)), dma((reach,)), dma((reach,)),
        ],
        compiler_params=pltpu.CompilerParams(
            collective_id=0, has_side_effects=True, vmem_limit_bytes=48 << 20),
        cost_estimate=pl.CostEstimate(
            flops=2 * channels * tokens * 1500, bytes_accessed=8 * channels * tokens, transcendentals=0),
    )(features, short_filter, mr_filter, mr_bias[None, :], candidate[None, :])


def solution(mesh):
    placed = (
        P(None, "tp", ("groups", "seq")),
        P(None, None, "tp"),
        P("tp", None),
        P("tp"),
        P(("groups", "seq")),
    )
    return jax.shard_map(
        on_device, mesh=mesh, in_specs=placed, out_specs=P("tp", ("groups", "seq")), check_vma=False
    )
```

```python
import functools

import jax
import jax.numpy as jnp
from jax import lax
from jax.experimental import pallas as pl
from jax.experimental.pallas import tpu as pltpu
from jax.sharding import PartitionSpec as P

NCAND = 4
ROWS = 128
LANES = 128
AT_ONCE = 8
PER = 2
WIDE = PER * ROWS
F32 = jnp.float32
BF16 = jnp.bfloat16


def iota(shape, dim):
    return lax.broadcasted_iota(jnp.int32, shape, dim)


def dot(a, b):
    return jnp.dot(a, b, preferred_element_type=F32)


def earlier_ids(ids, own):
    total = jnp.zeros(own.shape, jnp.int32)
    for cand in range(NCAND):
        fewer = jnp.sum((ids < cand).astype(F32), axis=1, keepdims=True).astype(jnp.int32)
        total = jnp.where(own == cand, fewer, total)
    return total


def kernel(
    count, reach,
    x_hbm, filt_hbm, mr_hbm, bias_hbm, cand_hbm, out_ref,
    x_ref, filt_ref, mr_ref, bias_ref, cand_ref, load_sem,
    rows_ref, prm_ref, mrf_ref, late_ref, early_ref, band_ref, pool_ref, table_ref,
    g0_ref, g1_ref, gh_ref, gate_ref, conv_ref, mixsum_ref,
    rim_out, rim_in, ids_in, sums_out, sums_in,
    halo_send, halo_recv, rim_send, rim_recv, ids_send, ids_recv, sums_send, sums_recv,
):
    me = lax.axis_index("seq")
    channels, tokens = out_ref.shape
    chunks = channels // ROWS
    groups = mr_ref.shape[0]
    size = channels // groups
    per_chunk = ROWS // size
    n_to = jnp.minimum(reach, count - 1 - me)
    n_from = jnp.minimum(reach, me)

    def halo_copy(i):
        rows = pl.ds(pl.multiple_of(i * ROWS, ROWS), ROWS)
        return pltpu.make_async_remote_copy(
            src_ref=g1_ref.at[rows], dst_ref=gh_ref.at[rows],
            send_sem=halo_send.at[i], recv_sem=halo_recv.at[i],
            device_id={"seq": me + 1}, device_id_type=pl.DeviceIdType.MESH)

    def rim_copy():
        return pltpu.make_async_remote_copy(
            src_ref=rim_out, dst_ref=rim_in, send_sem=rim_send, recv_sem=rim_recv,
            device_id={"seq": me + 1}, device_id_type=pl.DeviceIdType.MESH)

    def ids_copy(d):
        return pltpu.make_async_remote_copy(
            src_ref=cand_ref, dst_ref=ids_in.at[d - 1],
            send_sem=ids_send.at[d - 1], recv_sem=ids_recv.at[d - 1],
            device_id={"seq": me + d}, device_id_type=pl.DeviceIdType.MESH)

    def sums_copy(d):
        return pltpu.make_async_remote_copy(
            src_ref=sums_out, dst_ref=sums_in.at[d - 1],
            send_sem=sums_send.at[d - 1], recv_sem=sums_recv.at[d - 1],
            device_id={"seq": me + d}, device_id_type=pl.DeviceIdType.MESH)

    loads = [pltpu.make_async_copy(there, here, load_sem.at[i]) for i, (there, here) in enumerate((
        (cand_hbm, cand_ref), (x_hbm, x_ref), (filt_hbm, filt_ref), (bias_hbm, bias_ref), (mr_hbm, mr_ref)))]
    for load in loads:
        load.start()

    def loop(low, high, body):
        def step(i, carry):
            body(i)
            return carry
        lax.fori_loop(low, high, step, 0)

    barrier = pltpu.get_barrier_semaphore()
    loop(1, n_from + 1, lambda d: pl.semaphore_signal(
        barrier, inc=1, device_id={"seq": me - d}, device_id_type=pl.DeviceIdType.MESH))

    loads[0].wait()
    own = cand_ref[...]
    start = earlier_ids(own, own)
    k2, t2 = iota((tokens, tokens), 0), iota((tokens, tokens), 1)
    inside = k2 >= start
    band_ref[...] = (inside & (k2 <= t2) & (t2 - k2 < LANES)).astype(F32).astype(BF16)
    pool_ref[...] = (inside & (k2 <= t2)).astype(F32).astype(BF16)
    one = (inside & (k2 == t2 - 1)).astype(F32).astype(BF16)
    two = (inside & (k2 == t2 - 2)).astype(F32).astype(BF16)
    late_ref[...] = jnp.concatenate([one[:, LANES:], two[:, LANES:]], axis=1)
    early_ref[...] = jnp.concatenate([one[:LANES, :LANES], two[:LANES, :LANES]], axis=1)

    for load in loads[2:]:
        load.wait()
    rows_ref[...] = jnp.zeros_like(rows_ref)

    def turn(i):
        for u in range(PER):
            rows = pl.ds(pl.multiple_of(i * WIDE + u * ROWS, ROWS), ROWS)
            for j in range(3):
                rows_ref[u, 3 * j:3 * j + 3, :] = filt_ref[j, :, rows]
            rows_ref[u, 9:10, :] = bias_ref[:, rows]
        for u in range(PER):
            rows = pl.ds(pl.multiple_of(i * WIDE + u * ROWS, ROWS), ROWS)
            prm_ref[rows, :] = rows_ref[u].T

    loop(0, chunks // PER, turn)
    mrf_ref[...] = mr_ref[...].astype(F32)

    row_k, lane_k = iota((16, LANES), 0), iota((16, LANES), 1)
    rim = jnp.zeros((16, channels), F32)
    loads[1].wait()
    for b in range(3):
        pick = (lane_k - (LANES - 2) == row_k - 2 * b) & (lane_k >= LANES - 2)
        rim = rim + lax.dot_general(
            pick.astype(F32).astype(BF16), x_ref[b, :, tokens - LANES:],
            (((1,), (1,)), ((), ())), preferred_element_type=F32)
    rim_out[...] = rim.astype(BF16)

    @pl.when(me + 1 < count)
    def _():
        pl.semaphore_wait(barrier, n_to)

    loop(1, n_to + 1, lambda d: ids_copy(d).start())

    @pl.when(me + 1 < count)
    def _():
        rim_copy().start()

    def tail(i):
        many = [pl.ds(pl.multiple_of(i * WIDE + u * ROWS, ROWS), ROWS) for u in range(PER)]
        x = [x_ref[b, rows, :] for rows in many for b in (1, 2)]
        prm = [prm_ref[rows, :] for rows in many]
        lags = dot(jnp.concatenate(x, axis=0), late_ref[...])
        for u, rows in enumerate(many):
            outs = []
            for b in (1, 2):
                at = 2 * u + b - 1
                lag = lags[at * ROWS:(at + 1) * ROWS]
                outs.append(prm[u][:, b:b + 1] * x[at][:, LANES:].astype(F32)
                            + prm[u][:, 3 + b:4 + b] * lag[:, :LANES] + prm[u][:, 6 + b:7 + b] * lag[:, LANES:])
            g1_ref[rows, :] = (outs[0] * outs[1]).astype(BF16)

        @pl.when(me + 1 < count)
        def _():
            for u in range(PER):
                halo_copy(i * PER + u).start()

    loop(0, chunks // PER, tail)
    @pl.when(me == 0)
    def _():
        gh_ref[...] = jnp.zeros_like(gh_ref)
        rim_in[...] = jnp.zeros_like(rim_in)
        ids_in[0] = jnp.full(ids_in.shape[1:], -1, jnp.int32)

    @pl.when(me > 0)
    def _():
        rim_copy().wait_recv()
    loop(1, n_from + 1, lambda d: ids_copy(d).wait_recv())

    start_all = start + earlier_ids(ids_in[0][:, tokens - LANES:], own) - LANES
    kh, th = iota((LANES, LANES), 0), iota((LANES, LANES), 1)
    halo_mask = ((kh > th) & (kh - LANES >= start_all[:, :LANES])).astype(F32).astype(BF16)
    row_q, lane_q = iota((16, LANES), 0), iota((16, LANES), 1)

    def rim_pick(b, lag):
        token = row_q - 2 * b - 2
        hit = (token == lane_q - lag) & (token >= start_all[:, :LANES]) & (token < 0) & (token >= -2)
        return hit.astype(F32).astype(BF16)

    picks = [jnp.concatenate([rim_pick(b, 1), rim_pick(b, 2)], axis=1) for b in range(3)]

    def head(i):
        wide = pl.ds(pl.multiple_of(i * WIDE, WIDE), WIDE)
        x = [x_ref[b, wide, :] for b in range(3)]
        edge = rim_in[:, wide]
        lags = [dot(x[b][:, :LANES], early_ref[...]) + lax.dot_general(
            edge, picks[b], (((0,), (0,)), ((), ())), preferred_element_type=F32) for b in range(3)]
        late = dot(x[0], late_ref[...])
        prm = prm_ref[wide, :]

        def short(b, now, lag):
            return (prm[:, b:b + 1] * now.astype(F32)
                    + prm[:, 3 + b:4 + b] * lag[:, :LANES] + prm[:, 6 + b:7 + b] * lag[:, LANES:])

        g0_ref[wide, :] = (short(1, x[1][:, :LANES], lags[1]) * short(2, x[2][:, :LANES], lags[2])).astype(BF16)
        gate_ref[wide, :LANES] = short(0, x[0][:, :LANES], lags[0])
        gate_ref[wide, LANES:] = short(0, x[0][:, LANES:], late)

    loop(0, chunks // PER, head)

    def conv(i):
        some = [pl.ds(pl.multiple_of((i * AT_ONCE + u) * size, size), size) for u in range(AT_ONCE)]
        near = [g0_ref[rows, :] for rows in some]
        late = [g1_ref[rows, :] for rows in some]
        taps = [mrf_ref[pl.ds(i * AT_ONCE + u, 1), :] for u in range(AT_ONCE)]
        for u, rows in enumerate(some):
            wheel = pltpu.roll(
                jnp.broadcast_to(taps[u], (LANES, LANES)), 0, 1, stride=1, stride_axis=0).astype(BF16)
            table_ref[i * AT_ONCE + u] = wheel * halo_mask
            conv_ref[rows, :LANES] = dot(near[u], wheel * band_ref[:LANES, :LANES])
            conv_ref[rows, LANES:] = dot(
                jnp.concatenate([near[u], late[u]], axis=1),
                jnp.concatenate([wheel, wheel], axis=0) * band_ref[:, LANES:])

    loop(0, groups // AT_ONCE, conv)

    last = jnp.max(own.astype(F32), axis=1, keepdims=True)
    last_of = (iota((tokens, tokens), 0) >= earlier_ids(own, last.astype(jnp.int32)))
    last_col = last_of[:, :LANES].astype(F32)
    lane_p = iota((tokens, LANES), 1)
    mixsum_ref[...] = jnp.zeros_like(mixsum_ref)

    def mix(i):
        @pl.when(me > 0)
        def _():
            for u in range(PER):
                halo_copy(i * PER + u).wait_recv()

        wide = pl.ds(pl.multiple_of(i * WIDE, WIDE), WIDE)
        far = [dot(gh_ref[pl.ds(pl.multiple_of(i * WIDE + u * size, size), size), :], table_ref[i * (WIDE // size) + u])
               for u in range(WIDE // size)]
        bias = prm_ref[wide, 9:10]
        mixed = jnp.concatenate([
            (gate_ref[wide, :LANES] * (conv_ref[wide, :LANES] + jnp.concatenate(far, axis=0)
                                       + bias * g0_ref[wide, :].astype(F32))).astype(BF16),
            (gate_ref[wide, LANES:] * (conv_ref[wide, LANES:] + bias * g1_ref[wide, :].astype(F32))).astype(BF16),
        ], axis=1)
        conv_ref[wide, :] = dot(mixed, pool_ref[...])
        mixsum_ref[...] += sum(
            dot(mixed[u * ROWS:(u + 1) * ROWS], jnp.where(lane_p == i * PER + u, last_col, 0.0).astype(BF16))
            for u in range(PER))

    loop(0, chunks // PER, mix)

    sums_out[...] = mixsum_ref[...].T[:sums_out.shape[0], :]
    loop(1, n_to + 1, lambda d: sums_copy(d).start())

    first = jnp.min(own.astype(F32), axis=1, keepdims=True).astype(jnp.int32)
    mixsum_ref[...] = jnp.zeros_like(mixsum_ref)

    def gather(d, before):
        sums_copy(d).wait_recv()
        ids = ids_in[d - 1]
        same = jnp.max(ids.astype(F32), axis=1, keepdims=True).astype(jnp.int32) == first
        mixsum_ref[:sums_out.shape[0], :] += jnp.where(same, sums_in[d - 1], 0.0)
        return before + jnp.sum((ids == first).astype(F32), axis=1, keepdims=True)

    before = lax.fori_loop(1, n_from + 1, gather, jnp.zeros((1, 1), F32))
    carried = (start == 0).astype(F32)
    seen = (iota(start.shape, 1) + 1 - start).astype(F32) + carried * before
    scale = 1.0 / jnp.sqrt(seen)
    mixsum_ref[...] = mixsum_ref[...].T

    def finish(i):
        rows = pl.ds(pl.multiple_of(i * ROWS, ROWS), ROWS)
        column = jnp.sum(jnp.where(iota((ROWS, LANES), 1) == i, mixsum_ref[...], 0.0), axis=1, keepdims=True)
        out_ref[rows, :] = ((conv_ref[rows, :] + column * carried) * scale).astype(BF16)

    loop(0, chunks, finish)

    loop(1, n_to + 1, lambda d: sums_copy(d).wait_send())
    loop(1, n_to + 1, lambda d: ids_copy(d).wait_send())

    @pl.when(me + 1 < count)
    def _():
        rim_copy().wait_send()
        loop(0, chunks, lambda i: halo_copy(i).wait_send())


def on_device(features, short_filter, mr_filter, mr_bias, candidate):
    count = lax.axis_size("seq")
    reach = max(1, count // 2)
    _, channels, tokens = features.shape
    groups = mr_filter.shape[0]
    chunks = channels // ROWS
    sum_rows = -(-chunks // 8) * 8
    dma = pltpu.SemaphoreType.DMA
    vmem = pl.BlockSpec(memory_space=pltpu.VMEM)
    return pl.pallas_call(
        functools.partial(kernel, count, reach),
        out_shape=jax.ShapeDtypeStruct((channels, tokens), BF16),
        in_specs=[pl.BlockSpec(memory_space=pltpu.HBM)] * 5,
        out_specs=vmem,
        scratch_shapes=[
            pltpu.VMEM(features.shape, BF16),
            pltpu.VMEM(short_filter.shape, F32),
            pltpu.VMEM(mr_filter.shape, BF16),
            pltpu.VMEM((1, channels), F32),
            pltpu.VMEM((1, tokens), jnp.int32),
            dma((5,)),
            pltpu.VMEM((PER, ROWS, LANES), F32),
            pltpu.VMEM((channels, LANES), F32),
            pltpu.VMEM((groups, LANES), F32),
            pltpu.VMEM((tokens, tokens), BF16),
            pltpu.VMEM((LANES, tokens), BF16),
            pltpu.VMEM((tokens, tokens), BF16),
            pltpu.VMEM((tokens, tokens), BF16),
            pltpu.VMEM((groups, LANES, LANES), BF16),
            pltpu.VMEM((channels, LANES), BF16),
            pltpu.VMEM((channels, LANES), BF16),
            pltpu.VMEM((channels, LANES), BF16),
            pltpu.VMEM((channels, tokens), F32),
            pltpu.VMEM((channels, tokens), F32),
            pltpu.VMEM((LANES, LANES), F32),
            pltpu.VMEM((16, channels), BF16),
            pltpu.VMEM((16, channels), BF16),
            pltpu.VMEM((reach, 1, tokens), jnp.int32),
            pltpu.VMEM((sum_rows, LANES), F32),
            pltpu.VMEM((reach, sum_rows, LANES), F32),
            dma((chunks,)), dma((chunks,)), dma, dma,
            dma((reach,)), dma((reach,)), dma((reach,)), dma((reach,)),
        ],
        compiler_params=pltpu.CompilerParams(
            collective_id=0, has_side_effects=True, vmem_limit_bytes=60 << 20),
        cost_estimate=pl.CostEstimate(
            flops=2 * channels * tokens * 1500, bytes_accessed=8 * channels * tokens, transcendentals=0),
    )(features, short_filter, mr_filter, mr_bias[None, :], candidate[None, :])


def solution(mesh):
    placed = (
        P(None, "tp", ("groups", "seq")),
        P(None, None, "tp"),
        P("tp", None),
        P("tp"),
        P(("groups", "seq")),
    )
    return jax.shard_map(
        on_device, mesh=mesh, in_specs=placed, out_specs=P("tp", ("groups", "seq")), check_vma=False
    )
```

```python
import functools

import jax
import jax.numpy as jnp
from jax import lax
from jax.experimental import pallas as pl
from jax.experimental.pallas import tpu as pltpu
from jax.sharding import PartitionSpec as P

NCAND = 4
ROWS = 128
LANES = 128
AT_ONCE = 16
PER = 4
WIDE = PER * ROWS
F32 = jnp.float32
BF16 = jnp.bfloat16


def iota(shape, dim):
    return lax.broadcasted_iota(jnp.int32, shape, dim)


def dot(a, b):
    return jnp.dot(a, b, preferred_element_type=F32)


def earlier_ids(ids, own):
    total = jnp.zeros(own.shape, jnp.int32)
    for cand in range(NCAND):
        fewer = jnp.sum((ids < cand).astype(F32), axis=1, keepdims=True).astype(jnp.int32)
        total = jnp.where(own == cand, fewer, total)
    return total


def kernel(
    count, reach,
    x_hbm, filt_hbm, mr_hbm, bias_hbm, cand_hbm, out_ref,
    x_ref, filt_ref, mr_ref, bias_ref, cand_ref, load_sem,
    rows_ref, prm_ref, mrf_ref, late_ref, early_ref, band_ref, pool_ref, table_ref,
    g0_ref, g1_ref, gh_ref, gate_ref, conv_ref, mixsum_ref,
    rim_out, rim_in, picks_ref, ids_in, sums_out, sums_in,
    halo_send, halo_recv, rim_send, rim_recv, ids_send, ids_recv, sums_send, sums_recv,
):
    me = lax.axis_index("seq")
    channels, tokens = out_ref.shape
    chunks = channels // ROWS
    groups = mr_ref.shape[0]
    size = channels // groups
    per_chunk = ROWS // size
    n_to = jnp.minimum(reach, count - 1 - me)
    n_from = jnp.minimum(reach, me)

    def halo_copy(i):
        rows = pl.ds(pl.multiple_of(i * ROWS, ROWS), ROWS)
        return pltpu.make_async_remote_copy(
            src_ref=g1_ref.at[rows], dst_ref=gh_ref.at[rows],
            send_sem=halo_send.at[i], recv_sem=halo_recv.at[i],
            device_id={"seq": me + 1}, device_id_type=pl.DeviceIdType.MESH)

    def rim_copy():
        return pltpu.make_async_remote_copy(
            src_ref=rim_out, dst_ref=rim_in, send_sem=rim_send, recv_sem=rim_recv,
            device_id={"seq": me + 1}, device_id_type=pl.DeviceIdType.MESH)

    def ids_copy(d):
        return pltpu.make_async_remote_copy(
            src_ref=cand_ref, dst_ref=ids_in.at[d - 1],
            send_sem=ids_send.at[d - 1], recv_sem=ids_recv.at[d - 1],
            device_id={"seq": me + d}, device_id_type=pl.DeviceIdType.MESH)

    def sums_copy(d, half):
        return pltpu.make_async_remote_copy(
            src_ref=sums_out.at[half], dst_ref=sums_in.at[d - 1, half],
            send_sem=sums_send.at[d - 1, half], recv_sem=sums_recv.at[d - 1, half],
            device_id={"seq": me + d}, device_id_type=pl.DeviceIdType.MESH)

    loads = [pltpu.make_async_copy(there, here, load_sem.at[i]) for i, (there, here) in enumerate((
        (cand_hbm, cand_ref), (x_hbm, x_ref), (filt_hbm, filt_ref), (bias_hbm, bias_ref), (mr_hbm, mr_ref)))]
    for load in loads:
        load.start()

    def loop(low, high, body):
        def step(i, carry):
            body(i)
            return carry
        lax.fori_loop(low, high, step, 0)

    barrier = pltpu.get_barrier_semaphore()
    loop(1, n_from + 1, lambda d: pl.semaphore_signal(
        barrier, inc=1, device_id={"seq": me - d}, device_id_type=pl.DeviceIdType.MESH))

    loads[0].wait()
    own = cand_ref[...]
    start = earlier_ids(own, own)
    k2, t2 = iota((tokens, tokens), 0), iota((tokens, tokens), 1)
    inside = k2 >= start
    band_ref[...] = (inside & (k2 <= t2) & (t2 - k2 < LANES)).astype(F32).astype(BF16)
    pool_ref[...] = (inside & (k2 <= t2)).astype(F32).astype(BF16)
    one = (inside & (k2 == t2 - 1)).astype(F32).astype(BF16)
    two = (inside & (k2 == t2 - 2)).astype(F32).astype(BF16)
    late_ref[...] = jnp.concatenate([one[:, LANES:], two[:, LANES:]], axis=1)
    early_ref[...] = jnp.concatenate([one[:LANES, :LANES], two[:LANES, :LANES]], axis=1)

    for load in loads[2:]:
        load.wait()
    rows_ref[...] = jnp.zeros_like(rows_ref)

    def turn(i):
        for u in range(PER):
            rows = pl.ds(pl.multiple_of(i * WIDE + u * ROWS, ROWS), ROWS)
            for j in range(3):
                rows_ref[u, 3 * j:3 * j + 3, :] = filt_ref[j, :, rows]
            rows_ref[u, 9:10, :] = bias_ref[:, rows]
        for u in range(PER):
            rows = pl.ds(pl.multiple_of(i * WIDE + u * ROWS, ROWS), ROWS)
            prm_ref[rows, :] = rows_ref[u].T

    loop(0, chunks // PER, turn)
    mrf_ref[...] = mr_ref[...].astype(F32)

    row_k, lane_k = iota((16, LANES), 0), iota((16, LANES), 1)
    rim = jnp.zeros((16, channels // 2), F32)
    loads[1].wait()
    for half in range(2):
        for b in range(3):
            pick = (lane_k - (LANES - 2) == row_k - 8 * half - 2 * b) & (lane_k >= LANES - 2)
            rim = rim + lax.dot_general(
                pick.astype(F32).astype(BF16),
                x_ref[b, half * channels // 2:(half + 1) * channels // 2, tokens - LANES:],
                (((1,), (1,)), ((), ())), preferred_element_type=F32)
    rim_out[...] = rim.astype(BF16)

    @pl.when(me + 1 < count)
    def _():
        pl.semaphore_wait(barrier, n_to)

    loop(1, n_to + 1, lambda d: ids_copy(d).start())

    @pl.when(me + 1 < count)
    def _():
        rim_copy().start()

    def tail(i):
        many = [pl.ds(pl.multiple_of(i * WIDE + u * ROWS, ROWS), ROWS) for u in range(PER)]
        x = [x_ref[b, rows, :] for rows in many for b in (1, 2)]
        prm = [prm_ref[rows, :] for rows in many]
        lags = dot(jnp.concatenate(x, axis=0), late_ref[...])
        for u, rows in enumerate(many):
            outs = []
            for b in (1, 2):
                at = 2 * u + b - 1
                lag = lags[at * ROWS:(at + 1) * ROWS]
                outs.append(prm[u][:, b:b + 1] * x[at][:, LANES:].astype(F32)
                            + prm[u][:, 3 + b:4 + b] * lag[:, :LANES] + prm[u][:, 6 + b:7 + b] * lag[:, LANES:])
            g1_ref[rows, :] = (outs[0] * outs[1]).astype(BF16)

        @pl.when(me + 1 < count)
        def _():
            for u in range(PER):
                halo_copy(i * PER + u).start()

    loop(0, chunks // PER, tail)
    @pl.when(me == 0)
    def _():
        gh_ref[...] = jnp.zeros_like(gh_ref)
        rim_in[...] = jnp.zeros_like(rim_in)
        ids_in[0] = jnp.full(ids_in.shape[1:], -1, jnp.int32)

    @pl.when(me > 0)
    def _():
        rim_copy().wait_recv()
    loop(1, n_from + 1, lambda d: ids_copy(d).wait_recv())

    start_all = start + earlier_ids(ids_in[0][:, tokens - LANES:], own) - LANES
    first = jnp.min(own.astype(F32), axis=1, keepdims=True).astype(jnp.int32)
    before = lax.fori_loop(
        1, n_from + 1,
        lambda d, total: total + jnp.sum((ids_in[d - 1] == first).astype(F32), axis=1, keepdims=True),
        jnp.zeros((1, 1), F32))
    carried = (start == 0).astype(F32)
    scale = 1.0 / jnp.sqrt((iota(start.shape, 1) + 1 - start).astype(F32) + carried * before)
    carried = carried * scale

    kh, th = iota((LANES, LANES), 0), iota((LANES, LANES), 1)
    halo_mask = ((kh > th) & (kh - LANES >= start_all[:, :LANES])).astype(F32).astype(BF16)
    row_q, lane_q = iota((16, LANES), 0), iota((16, LANES), 1)

    def rim_pick(half, b, lag):
        token = row_q - 8 * half - 2 * b - 2
        hit = (token == lane_q - lag) & (token >= start_all[:, :LANES]) & (token < 0) & (token >= -2)
        return hit.astype(F32).astype(BF16)

    for half in range(2):
        for b in range(3):
            picks_ref[half, b] = jnp.concatenate([rim_pick(half, b, 1), rim_pick(half, b, 2)], axis=1)
    half_steps = chunks // PER // 2

    def head(i):
        wide = pl.ds(pl.multiple_of(i * WIDE, WIDE), WIDE)
        x = [x_ref[b, wide, :] for b in range(3)]
        half = i // half_steps
        edge = rim_in[:, pl.ds(pl.multiple_of((i - half * half_steps) * WIDE, WIDE), WIDE)]
        lags = [dot(x[b][:, :LANES], early_ref[...]) + lax.dot_general(
            edge, picks_ref[half, b], (((0,), (0,)), ((), ())), preferred_element_type=F32) for b in range(3)]
        late = dot(x[0], late_ref[...])
        prm = prm_ref[wide, :]

        def short(b, now, lag):
            return (prm[:, b:b + 1] * now.astype(F32)
                    + prm[:, 3 + b:4 + b] * lag[:, :LANES] + prm[:, 6 + b:7 + b] * lag[:, LANES:])

        g0_ref[wide, :] = (short(1, x[1][:, :LANES], lags[1]) * short(2, x[2][:, :LANES], lags[2])).astype(BF16)
        gate_ref[wide, :LANES] = short(0, x[0][:, :LANES], lags[0])
        gate_ref[wide, LANES:] = short(0, x[0][:, LANES:], late)

    loop(0, chunks // PER, head)

    def conv(i):
        some = [pl.ds(pl.multiple_of((i * AT_ONCE + u) * size, size), size) for u in range(AT_ONCE)]
        near = [g0_ref[rows, :] for rows in some]
        late = [g1_ref[rows, :] for rows in some]
        taps = [mrf_ref[pl.ds(i * AT_ONCE + u, 1), :] for u in range(AT_ONCE)]
        for u, rows in enumerate(some):
            wheel = pltpu.roll(
                jnp.broadcast_to(taps[u], (LANES, LANES)), 0, 1, stride=1, stride_axis=0).astype(BF16)
            table_ref[i * AT_ONCE + u] = wheel * halo_mask
            conv_ref[rows, :LANES] = dot(near[u], wheel * band_ref[:LANES, :LANES])
            conv_ref[rows, LANES:] = dot(
                jnp.concatenate([near[u], late[u]], axis=1),
                jnp.concatenate([wheel, wheel], axis=0) * band_ref[:, LANES:])

    loop(0, groups // AT_ONCE, conv)

    lane_p = iota((ROWS, LANES), 1)
    mixsum_ref[...] = jnp.zeros_like(mixsum_ref)

    def mix(i):
        @pl.when(me > 0)
        def _():
            for u in range(PER):
                halo_copy(i * PER + u).wait_recv()

        wide = pl.ds(pl.multiple_of(i * WIDE, WIDE), WIDE)
        far = [dot(gh_ref[pl.ds(pl.multiple_of(i * WIDE + u * size, size), size), :], table_ref[i * (WIDE // size) + u])
               for u in range(WIDE // size)]
        bias = prm_ref[wide, 9:10]
        mixed = jnp.concatenate([
            (gate_ref[wide, :LANES] * (conv_ref[wide, :LANES] + jnp.concatenate(far, axis=0)
                                       + bias * g0_ref[wide, :].astype(F32))).astype(BF16),
            (gate_ref[wide, LANES:] * (conv_ref[wide, LANES:] + bias * g1_ref[wide, :].astype(F32))).astype(BF16),
        ], axis=1)
        local = dot(mixed, pool_ref[...])
        conv_ref[wide, :] = local
        half = i // half_steps
        kept = mixsum_ref[half]
        for u in range(PER):
            kept = jnp.where(lane_p == (i - half * half_steps) * PER + u,
                             local[u * ROWS:(u + 1) * ROWS, tokens - 1:], kept)
        mixsum_ref[half] = kept

    sum_rows = sums_out.shape[1]
    for half in range(2):
        loop(half * half_steps, (half + 1) * half_steps, mix)
        sums_out[half] = mixsum_ref[half].T[:sum_rows, :]
        loop(1, n_to + 1, lambda d: sums_copy(d, half).start())

    here = chunks // 2
    mixsum_ref[...] = jnp.zeros_like(mixsum_ref)
    for half in range(2):

        def gather(d):
            sums_copy(d, half).wait_recv()
            same = jnp.max(ids_in[d - 1].astype(F32), axis=1, keepdims=True).astype(jnp.int32) == first
            mixsum_ref[half, :sum_rows, :] += jnp.where(same, sums_in[d - 1, half], 0.0)

        loop(1, n_from + 1, gather)
        columns = mixsum_ref[half].T
        for i in range(here):
            rows = pl.ds((half * here + i) * ROWS, ROWS)
            out_ref[rows, :] = (conv_ref[rows, :] * scale + columns[:, i:i + 1] * carried).astype(BF16)

    for half in range(2):
        loop(1, n_to + 1, lambda d: sums_copy(d, half).wait_send())
    loop(1, n_to + 1, lambda d: ids_copy(d).wait_send())

    @pl.when(me + 1 < count)
    def _():
        rim_copy().wait_send()
        loop(0, chunks, lambda i: halo_copy(i).wait_send())


def on_device(features, short_filter, mr_filter, mr_bias, candidate):
    count = lax.axis_size("seq")
    reach = max(1, count // 2)
    _, channels, tokens = features.shape
    groups = mr_filter.shape[0]
    chunks = channels // ROWS
    sum_rows = -(-chunks // 16) * 8
    dma = pltpu.SemaphoreType.DMA
    vmem = pl.BlockSpec(memory_space=pltpu.VMEM)
    return pl.pallas_call(
        functools.partial(kernel, count, reach),
        out_shape=jax.ShapeDtypeStruct((channels, tokens), BF16),
        in_specs=[pl.BlockSpec(memory_space=pltpu.HBM)] * 5,
        out_specs=vmem,
        scratch_shapes=[
            pltpu.VMEM(features.shape, BF16),
            pltpu.VMEM(short_filter.shape, F32),
            pltpu.VMEM(mr_filter.shape, BF16),
            pltpu.VMEM((1, channels), F32),
            pltpu.VMEM((1, tokens), jnp.int32),
            dma((5,)),
            pltpu.VMEM((PER, ROWS, LANES), F32),
            pltpu.VMEM((channels, LANES), F32),
            pltpu.VMEM((groups, LANES), F32),
            pltpu.VMEM((tokens, tokens), BF16),
            pltpu.VMEM((LANES, tokens), BF16),
            pltpu.VMEM((tokens, tokens), BF16),
            pltpu.VMEM((tokens, tokens), BF16),
            pltpu.VMEM((groups, LANES, LANES), BF16),
            pltpu.VMEM((channels, LANES), BF16),
            pltpu.VMEM((channels, LANES), BF16),
            pltpu.VMEM((channels, LANES), BF16),
            pltpu.VMEM((channels, tokens), F32),
            pltpu.VMEM((channels, tokens), F32),
            pltpu.VMEM((2, LANES, LANES), F32),
            pltpu.VMEM((16, channels // 2), BF16),
            pltpu.VMEM((16, channels // 2), BF16),
            pltpu.VMEM((2, 3, 16, tokens), BF16),
            pltpu.VMEM((reach, 1, tokens), jnp.int32),
            pltpu.VMEM((2, sum_rows, LANES), F32),
            pltpu.VMEM((reach, 2, sum_rows, LANES), F32),
            dma((chunks,)), dma((chunks,)), dma, dma,
            dma((reach,)), dma((reach,)), dma((reach, 2)), dma((reach, 2)),
        ],
        compiler_params=pltpu.CompilerParams(
            collective_id=0, has_side_effects=True, vmem_limit_bytes=60 << 20),
        cost_estimate=pl.CostEstimate(
            flops=2 * channels * tokens * 1500, bytes_accessed=8 * channels * tokens, transcendentals=0),
    )(features, short_filter, mr_filter, mr_bias[None, :], candidate[None, :])


def solution(mesh):
    placed = (
        P(None, "tp", ("groups", "seq")),
        P(None, None, "tp"),
        P("tp", None),
        P("tp"),
        P(("groups", "seq")),
    )
    return jax.shard_map(
        on_device, mesh=mesh, in_specs=placed, out_specs=P("tp", ("groups", "seq")), check_vma=False
    )
```

```python
import functools

import jax
import jax.numpy as jnp
from jax import lax
from jax.experimental import pallas as pl
from jax.experimental.pallas import tpu as pltpu
from jax.sharding import PartitionSpec as P

NCAND = 4
ROWS = 128
LANES = 128
AT_ONCE = 16
PER = 4
WIDE = PER * ROWS
F32 = jnp.float32
BF16 = jnp.bfloat16


def iota(shape, dim):
    return lax.broadcasted_iota(jnp.int32, shape, dim)


def dot(a, b):
    return jnp.dot(a, b, preferred_element_type=F32)


def earlier_ids(ids, own):
    total = jnp.zeros(own.shape, jnp.int32)
    for cand in range(NCAND):
        fewer = jnp.sum((ids < cand).astype(F32), axis=1, keepdims=True).astype(jnp.int32)
        total = jnp.where(own == cand, fewer, total)
    return total


def kernel(
    count, reach,
    x_hbm, filt_hbm, mr_hbm, bias_hbm, cand_hbm, out_ref,
    x_ref, filt_ref, mr_ref, bias_ref, cand_ref, load_sem,
    rows_ref, prm_ref, mrf_ref, late_ref, early_ref, band_ref, pool_ref, table_ref,
    g0_ref, g1_ref, gh_ref, gate_ref, conv_ref, mixsum_ref,
    rim_out, rim_in, picks_ref, ids_in, sums_out, sums_in,
    halo_send, halo_recv, rim_send, rim_recv, ids_send, ids_recv, sums_send, sums_recv,
):
    me = lax.axis_index("seq")
    channels, tokens = out_ref.shape
    chunks = channels // ROWS
    groups = mr_ref.shape[0]
    size = channels // groups
    per_chunk = ROWS // size
    n_to = jnp.minimum(reach, count - 1 - me)
    n_from = jnp.minimum(reach, me)

    def halo_copy(i):
        rows = pl.ds(pl.multiple_of(i * ROWS, ROWS), ROWS)
        return pltpu.make_async_remote_copy(
            src_ref=g1_ref.at[rows], dst_ref=gh_ref.at[rows],
            send_sem=halo_send.at[i], recv_sem=halo_recv.at[i],
            device_id={"seq": me + 1}, device_id_type=pl.DeviceIdType.MESH)

    def rim_copy():
        return pltpu.make_async_remote_copy(
            src_ref=rim_out, dst_ref=rim_in, send_sem=rim_send, recv_sem=rim_recv,
            device_id={"seq": me + 1}, device_id_type=pl.DeviceIdType.MESH)

    def ids_copy(d):
        return pltpu.make_async_remote_copy(
            src_ref=cand_ref, dst_ref=ids_in.at[d - 1],
            send_sem=ids_send.at[d - 1], recv_sem=ids_recv.at[d - 1],
            device_id={"seq": me + d}, device_id_type=pl.DeviceIdType.MESH)

    def sums_copy(d, half):
        return pltpu.make_async_remote_copy(
            src_ref=sums_out.at[half], dst_ref=sums_in.at[d - 1, half],
            send_sem=sums_send.at[d - 1, half], recv_sem=sums_recv.at[d - 1, half],
            device_id={"seq": me + d}, device_id_type=pl.DeviceIdType.MESH)

    loads = [pltpu.make_async_copy(there, here, load_sem.at[i]) for i, (there, here) in enumerate((
        (cand_hbm, cand_ref), (x_hbm, x_ref), (filt_hbm, filt_ref), (bias_hbm, bias_ref), (mr_hbm, mr_ref)))]
    for at in (0, 2, 3, 1, 4):
        loads[at].start()

    def loop(low, high, body):
        def step(i, carry):
            body(i)
            return carry
        lax.fori_loop(low, high, step, 0)

    barrier = pltpu.get_barrier_semaphore()
    loop(1, n_from + 1, lambda d: pl.semaphore_signal(
        barrier, inc=1, device_id={"seq": me - d}, device_id_type=pl.DeviceIdType.MESH))

    loads[0].wait()
    own = cand_ref[...]
    start = earlier_ids(own, own)
    k2, t2 = iota((tokens, tokens), 0), iota((tokens, tokens), 1)
    inside = k2 >= start
    band_ref[...] = (inside & (k2 <= t2) & (t2 - k2 < LANES)).astype(F32).astype(BF16)
    pool_ref[...] = (inside & (k2 <= t2)).astype(F32).astype(BF16)
    one = (inside & (k2 == t2 - 1)).astype(F32).astype(BF16)
    two = (inside & (k2 == t2 - 2)).astype(F32).astype(BF16)
    late_ref[...] = jnp.concatenate([one[:, LANES:], two[:, LANES:]], axis=1)
    early_ref[...] = jnp.concatenate([one[:LANES, :LANES], two[:LANES, :LANES]], axis=1)

    loads[2].wait()
    loads[3].wait()
    rows_ref[...] = jnp.zeros_like(rows_ref)

    def turn(i):
        for u in range(PER):
            rows = pl.ds(pl.multiple_of(i * WIDE + u * ROWS, ROWS), ROWS)
            for j in range(3):
                rows_ref[u, 3 * j:3 * j + 3, :] = filt_ref[j, :, rows]
            rows_ref[u, 9:10, :] = bias_ref[:, rows]
        for u in range(PER):
            rows = pl.ds(pl.multiple_of(i * WIDE + u * ROWS, ROWS), ROWS)
            prm_ref[rows, :] = rows_ref[u].T

    loop(0, chunks // PER, turn)

    row_k, lane_k = iota((16, LANES), 0), iota((16, LANES), 1)
    rim = jnp.zeros((16, channels // 2), F32)
    loads[1].wait()
    for half in range(2):
        for b in range(3):
            pick = (lane_k - (LANES - 2) == row_k - 8 * half - 2 * b) & (lane_k >= LANES - 2)
            rim = rim + lax.dot_general(
                pick.astype(F32).astype(BF16),
                x_ref[b, half * channels // 2:(half + 1) * channels // 2, tokens - LANES:],
                (((1,), (1,)), ((), ())), preferred_element_type=F32)
    rim_out[...] = rim.astype(BF16)

    @pl.when(me + 1 < count)
    def _():
        pl.semaphore_wait(barrier, n_to)

    loop(1, n_to + 1, lambda d: ids_copy(d).start())

    @pl.when(me + 1 < count)
    def _():
        rim_copy().start()

    def tail(i):
        many = [pl.ds(pl.multiple_of(i * WIDE + u * ROWS, ROWS), ROWS) for u in range(PER)]
        x = [x_ref[b, rows, :] for rows in many for b in (1, 2)]
        prm = [prm_ref[rows, :] for rows in many]
        lags = dot(jnp.concatenate(x, axis=0), late_ref[...])
        for u, rows in enumerate(many):
            outs = []
            for b in (1, 2):
                at = 2 * u + b - 1
                lag = lags[at * ROWS:(at + 1) * ROWS]
                outs.append(prm[u][:, b:b + 1] * x[at][:, LANES:].astype(F32)
                            + prm[u][:, 3 + b:4 + b] * lag[:, :LANES] + prm[u][:, 6 + b:7 + b] * lag[:, LANES:])
            g1_ref[rows, :] = (outs[0] * outs[1]).astype(BF16)

        @pl.when(me + 1 < count)
        def _():
            for u in range(PER):
                halo_copy(i * PER + u).start()

    loop(0, chunks // PER, tail)
    loads[4].wait()
    mrf_ref[...] = mr_ref[...].astype(F32)

    @pl.when(me == 0)
    def _():
        gh_ref[...] = jnp.zeros_like(gh_ref)
        rim_in[...] = jnp.zeros_like(rim_in)
        ids_in[0] = jnp.full(ids_in.shape[1:], -1, jnp.int32)

    @pl.when(me > 0)
    def _():
        rim_copy().wait_recv()
    loop(1, n_from + 1, lambda d: ids_copy(d).wait_recv())

    start_all = start + earlier_ids(ids_in[0][:, tokens - LANES:], own) - LANES
    first = jnp.min(own.astype(F32), axis=1, keepdims=True).astype(jnp.int32)
    before = lax.fori_loop(
        1, n_from + 1,
        lambda d, total: total + jnp.sum((ids_in[d - 1] == first).astype(F32), axis=1, keepdims=True),
        jnp.zeros((1, 1), F32))
    carried = (start == 0).astype(F32)
    scale = 1.0 / jnp.sqrt((iota(start.shape, 1) + 1 - start).astype(F32) + carried * before)
    carried = carried * scale

    kh, th = iota((LANES, LANES), 0), iota((LANES, LANES), 1)
    halo_mask = ((kh > th) & (kh - LANES >= start_all[:, :LANES])).astype(F32).astype(BF16)
    row_q, lane_q = iota((16, LANES), 0), iota((16, LANES), 1)

    def rim_pick(half, b, lag):
        token = row_q - 8 * half - 2 * b - 2
        hit = (token == lane_q - lag) & (token >= start_all[:, :LANES]) & (token < 0) & (token >= -2)
        return hit.astype(F32).astype(BF16)

    for half in range(2):
        for b in range(3):
            picks_ref[half, b] = jnp.concatenate([rim_pick(half, b, 1), rim_pick(half, b, 2)], axis=1)
    half_steps = chunks // PER // 2

    def head(i):
        wide = pl.ds(pl.multiple_of(i * WIDE, WIDE), WIDE)
        x = [x_ref[b, wide, :] for b in range(3)]
        half = i // half_steps
        edge = rim_in[:, pl.ds(pl.multiple_of((i - half * half_steps) * WIDE, WIDE), WIDE)]
        lags = [dot(x[b][:, :LANES], early_ref[...]) + lax.dot_general(
            edge, picks_ref[half, b], (((0,), (0,)), ((), ())), preferred_element_type=F32) for b in range(3)]
        late = dot(x[0], late_ref[...])
        prm = prm_ref[wide, :]

        def short(b, now, lag):
            return (prm[:, b:b + 1] * now.astype(F32)
                    + prm[:, 3 + b:4 + b] * lag[:, :LANES] + prm[:, 6 + b:7 + b] * lag[:, LANES:])

        g0_ref[wide, :] = (short(1, x[1][:, :LANES], lags[1]) * short(2, x[2][:, :LANES], lags[2])).astype(BF16)
        gate_ref[wide, :LANES] = short(0, x[0][:, :LANES], lags[0])
        gate_ref[wide, LANES:] = short(0, x[0][:, LANES:], late)

    loop(0, chunks // PER, head)

    def conv(i):
        some = [pl.ds(pl.multiple_of((i * AT_ONCE + u) * size, size), size) for u in range(AT_ONCE)]
        near = [g0_ref[rows, :] for rows in some]
        late = [g1_ref[rows, :] for rows in some]
        taps = [mrf_ref[pl.ds(i * AT_ONCE + u, 1), :] for u in range(AT_ONCE)]
        for u, rows in enumerate(some):
            wheel = pltpu.roll(
                jnp.broadcast_to(taps[u], (LANES, LANES)), 0, 1, stride=1, stride_axis=0).astype(BF16)
            table_ref[i * AT_ONCE + u] = wheel * halo_mask
            conv_ref[rows, :LANES] = dot(near[u], wheel * band_ref[:LANES, :LANES])
            conv_ref[rows, LANES:] = dot(
                jnp.concatenate([near[u], late[u]], axis=1),
                jnp.concatenate([wheel, wheel], axis=0) * band_ref[:, LANES:])

    loop(0, groups // AT_ONCE, conv)

    lane_p = iota((ROWS, LANES), 1)
    mixsum_ref[...] = jnp.zeros_like(mixsum_ref)

    def mix(i):
        @pl.when(me > 0)
        def _():
            for u in range(PER):
                halo_copy(i * PER + u).wait_recv()

        wide = pl.ds(pl.multiple_of(i * WIDE, WIDE), WIDE)
        far = [dot(gh_ref[pl.ds(pl.multiple_of(i * WIDE + u * size, size), size), :], table_ref[i * (WIDE // size) + u])
               for u in range(WIDE // size)]
        bias = prm_ref[wide, 9:10]
        mixed = jnp.concatenate([
            (gate_ref[wide, :LANES] * (conv_ref[wide, :LANES] + jnp.concatenate(far, axis=0)
                                       + bias * g0_ref[wide, :].astype(F32))).astype(BF16),
            (gate_ref[wide, LANES:] * (conv_ref[wide, LANES:] + bias * g1_ref[wide, :].astype(F32))).astype(BF16),
        ], axis=1)
        local = dot(mixed, pool_ref[...])
        conv_ref[wide, :] = local
        half = i // half_steps
        kept = mixsum_ref[half]
        for u in range(PER):
            kept = jnp.where(lane_p == (i - half * half_steps) * PER + u,
                             local[u * ROWS:(u + 1) * ROWS, tokens - 1:], kept)
        mixsum_ref[half] = kept

    sum_rows = sums_out.shape[1]
    for half in range(2):
        loop(half * half_steps, (half + 1) * half_steps, mix)
        sums_out[half] = mixsum_ref[half].T[:sum_rows, :]
        loop(1, n_to + 1, lambda d: sums_copy(d, half).start())

    here = chunks // 2
    mixsum_ref[...] = jnp.zeros_like(mixsum_ref)
    for half in range(2):

        def gather(d):
            sums_copy(d, half).wait_recv()
            same = jnp.max(ids_in[d - 1].astype(F32), axis=1, keepdims=True).astype(jnp.int32) == first
            mixsum_ref[half, :sum_rows, :] += jnp.where(same, sums_in[d - 1, half], 0.0)

        loop(1, n_from + 1, gather)
        columns = mixsum_ref[half].T
        for i in range(here):
            rows = pl.ds((half * here + i) * ROWS, ROWS)
            out_ref[rows, :] = (conv_ref[rows, :] * scale + columns[:, i:i + 1] * carried).astype(BF16)

    for half in range(2):
        loop(1, n_to + 1, lambda d: sums_copy(d, half).wait_send())
    loop(1, n_to + 1, lambda d: ids_copy(d).wait_send())

    @pl.when(me + 1 < count)
    def _():
        rim_copy().wait_send()
        loop(0, chunks, lambda i: halo_copy(i).wait_send())


def on_device(features, short_filter, mr_filter, mr_bias, candidate):
    count = lax.axis_size("seq")
    reach = max(1, count // 2)
    _, channels, tokens = features.shape
    groups = mr_filter.shape[0]
    chunks = channels // ROWS
    sum_rows = -(-chunks // 16) * 8
    dma = pltpu.SemaphoreType.DMA
    vmem = pl.BlockSpec(memory_space=pltpu.VMEM)
    return pl.pallas_call(
        functools.partial(kernel, count, reach),
        out_shape=jax.ShapeDtypeStruct((channels, tokens), BF16),
        in_specs=[pl.BlockSpec(memory_space=pltpu.HBM)] * 5,
        out_specs=vmem,
        scratch_shapes=[
            pltpu.VMEM(features.shape, BF16),
            pltpu.VMEM(short_filter.shape, F32),
            pltpu.VMEM(mr_filter.shape, BF16),
            pltpu.VMEM((1, channels), F32),
            pltpu.VMEM((1, tokens), jnp.int32),
            dma((5,)),
            pltpu.VMEM((PER, ROWS, LANES), F32),
            pltpu.VMEM((channels, LANES), F32),
            pltpu.VMEM((groups, LANES), F32),
            pltpu.VMEM((tokens, tokens), BF16),
            pltpu.VMEM((LANES, tokens), BF16),
            pltpu.VMEM((tokens, tokens), BF16),
            pltpu.VMEM((tokens, tokens), BF16),
            pltpu.VMEM((groups, LANES, LANES), BF16),
            pltpu.VMEM((channels, LANES), BF16),
            pltpu.VMEM((channels, LANES), BF16),
            pltpu.VMEM((channels, LANES), BF16),
            pltpu.VMEM((channels, tokens), F32),
            pltpu.VMEM((channels, tokens), F32),
            pltpu.VMEM((2, LANES, LANES), F32),
            pltpu.VMEM((16, channels // 2), BF16),
            pltpu.VMEM((16, channels // 2), BF16),
            pltpu.VMEM((2, 3, 16, tokens), BF16),
            pltpu.VMEM((reach, 1, tokens), jnp.int32),
            pltpu.VMEM((2, sum_rows, LANES), F32),
            pltpu.VMEM((reach, 2, sum_rows, LANES), F32),
            dma((chunks,)), dma((chunks,)), dma, dma,
            dma((reach,)), dma((reach,)), dma((reach, 2)), dma((reach, 2)),
        ],
        compiler_params=pltpu.CompilerParams(
            collective_id=0, has_side_effects=True, vmem_limit_bytes=60 << 20),
        cost_estimate=pl.CostEstimate(
            flops=2 * channels * tokens * 1500, bytes_accessed=8 * channels * tokens, transcendentals=0),
    )(features, short_filter, mr_filter, mr_bias[None, :], candidate[None, :])


def solution(mesh):
    placed = (
        P(None, "tp", ("groups", "seq")),
        P(None, None, "tp"),
        P("tp", None),
        P("tp"),
        P(("groups", "seq")),
    )
    return jax.shard_map(
        on_device, mesh=mesh, in_specs=placed, out_specs=P("tp", ("groups", "seq")), check_vma=False
    )
```
